1024 devices in a mesh: ctx: 64 (over z_lo, y, core), tp: 16 (over x, z_hi).
Axes of the slice: x: 4, y: 4, z: 32 (z_hi: 4, z_lo: 8; z = z_hi * 8 + z_lo), core: 2. Of those that a mesh axis runs over, the one named last changes fastest.
Arguments:
- queries: bfloat16 [65536, 4096], P('ctx', 'tp'), may hold values from -6 to 6
- keys: bfloat16 [65536, 4096], P('ctx', 'tp'), may hold values from -6 to 6
- values: bfloat16 [65536, 4096], P('ctx', 'tp'), may hold values from -6 to 6
- residues: float32 [16, 4096], P(None, 'tp'), may hold values from -4 to 4
- rates: float32 [16, 4096], P(None, 'tp'), may hold values from 3.8146973e-06 to 0.04
- out_weight: bfloat16 [4096, 4096], P('tp'), may hold values from -0.125 to 0.125
- span_order: int32 [128], replicated, may hold values from 0 to 127, each once
Outputs:
- projected: bfloat16 [65536, 4096], P('ctx', 'tp')
The draws below stay inside these ranges and needn't reach their ends.
Inputs may be any that keep to these rules, and one draw needn't show every extreme that they name: span_order holds each of 0 .. 127 once.
All inputs are finite; a program needn't handle non-finite values.
Results may differ from the reference program's by a relative error of at most 0.015.
Values may be sent and summed in bfloat16 or wider, within the bound.
A program may use at most 32 MiB of HBM per device.

```python
import math
import jax
import jax.numpy as jnp
from jax import lax

D = 4096
MODES = 16
BLK = 64
SEQ = 65536
NCHUNK = 128
N_TP = 16


def with_spikes(result, own_key, source, target, parts, factor):
    owner, partner = [(jnp.arange(result.shape[axis_at]) // (result.shape[axis_at] // parts)).reshape([-1 if axis == axis_at else 1 for axis in range(result.ndim)]) for axis_at in (source, target)]
    chosen = jax.random.permutation(own_key, parts)[partner]
    strong = (owner == chosen) | (owner == (partner + parts // 2) % parts)
    return jnp.where(strong, factor * result, result)


def block_levels(own_key, shape, split, smallest, top_value):
    loudness, own = 1.0, jax.random.fold_in(own_key, 6)
    for position, blocks in split:
        steps = jnp.exp(jax.random.uniform(jax.random.fold_in(own, position), (blocks,), jnp.float32, smallest / len(split), top_value / len(split)))
        loudness = loudness * jnp.repeat(steps, shape[position] // blocks).reshape([-1 if axis == position else 1 for axis in range(len(shape))])
    return loudness


def centred(own_key, dims, deviation, limit, cuts=(), held_as=jnp.bfloat16):
    drawn = jax.random.normal(own_key, dims, jnp.float32) * deviation
    if len(cuts) > 0:
        drawn = block_levels(own_key, dims, cuts, -0.22, 0.18) * drawn
    return jnp.clip(drawn, min=-limit, max=limit).astype(held_as)


def bell_draw_with(key, extent, scale, most, shards, heavy, held_as=jnp.bfloat16):
    drawn = scale * jax.random.normal(key, extent, jnp.float32)
    if shards:
        drawn = drawn * block_levels(key, extent, shards, -0.22, 0.18)
    return jnp.clip(with_spikes(drawn, jax.random.fold_in(key, 3), *heavy), -most, most).astype(held_as)


def setup_inputs(seed: int = 0) -> dict:
    key_list = jax.random.split(jax.random.key(seed), 8)
    return {
        "queries": centred(key_list[0], (SEQ, D), 1.0, 6.0, ((0, 64), (1, 16))),
        "keys": centred(key_list[1], (SEQ, D), 1.0, 6.0, ((0, 64), (1, 16))),
        "values": centred(key_list[2], (SEQ, D), 1.0, 6.0, ((0, 64), (1, 16))),
        "residues": centred(key_list[3], (MODES, D), 0.25, 4.0, ((1, 16),), jnp.float32),
        "rates": jnp.clip(jnp.exp(math.log(0.04) - 9.257773 * jax.random.uniform(key_list[4], (MODES, D), jnp.float32) ** block_levels(key_list[4], (MODES, D), ((1, 16),), -0.2, 0.2)), 3.814697265625e-06, 0.04),
        "out_weight": bell_draw_with(key_list[5], (D, D), D ** -0.5, 0.125, ((0, 16),), (0, 1, 16, 2.0)),
        "span_order": jax.random.permutation(key_list[6], NCHUNK).astype(jnp.int32),
    }


def channel_mix(ordered, residues, rates):
    seq_len, width_all = ordered.shape
    group = width_all // N_TP
    nblocks = seq_len // BLK

    def one_group(index):
        start = (index * group).astype(jnp.int32)
        signal = lax.dynamic_slice_in_dim(ordered, start, group, 1).astype(jnp.float32)
        weights = lax.dynamic_slice_in_dim(residues, start, group, 1)
        decays = lax.dynamic_slice_in_dim(rates, start, group, 1)
        scaled = weights * jnp.sqrt(2.0 * decays)
        lags = jnp.arange(BLK).astype(jnp.float32)
        kernel = lax.optimization_barrier(jnp.sum(scaled[:, None, :] * jnp.exp(-decays[:, None, :] * lags[None, :, None]), axis=0))
        spread = jnp.arange(BLK)[:, None] - jnp.arange(BLK)[None, :]
        toeplitz = jnp.where((spread >= 0)[:, :, None], kernel[jnp.maximum(spread, 0)], 0.0)
        blocks = signal.reshape(nblocks, BLK, group)
        inner = jnp.einsum('tsc,nsc->ntc', toeplitz, blocks, precision=lax.Precision.HIGHEST)
        falling = jnp.exp(-decays[:, None, :] * (BLK - 1.0 - lags)[None, :, None])
        states = jnp.einsum('nsc,rsc->nrc', blocks, falling, precision=lax.Precision.HIGHEST)
        step_decay = jnp.exp(-decays * BLK)

        def advance(carry, state):
            return (step_decay * carry + state, carry)
        initial = jnp.zeros(decays.shape, jnp.float32)
        final_state, entering = lax.scan(advance, initial, states)
        rising = scaled[:, None, :] * jnp.exp(-decays[:, None, :] * (lags + 1.0)[None, :, None])
        outer = jnp.einsum('nrc,rtc->ntc', entering, rising, precision=lax.Precision.HIGHEST)
        return (inner + outer).reshape(seq_len, group)
    results = lax.map(one_group, jnp.arange(N_TP).astype(jnp.int32))
    return jnp.transpose(results, (1, 0, 2)).reshape(seq_len, width_all)

def reference(queries, keys, values, residues, rates, out_weight, span_order):
    seq_len, width_all = queries.shape
    count = span_order.shape[0]
    block_rows = seq_len // count
    gated = (keys.astype(jnp.float32) * values.astype(jnp.float32)).astype(jnp.bfloat16)
    inverse = jnp.argsort(span_order).astype(jnp.int32)
    ordered = gated.reshape(count, block_rows, width_all)[inverse].reshape(seq_len, width_all)
    convolved = channel_mix(ordered, residues, rates).astype(jnp.bfloat16)
    mixed = convolved.reshape(count, block_rows, width_all)[span_order.astype(jnp.int32)].reshape(seq_len, width_all)
    output = (queries.astype(jnp.float32) * mixed.astype(jnp.float32)).astype(jnp.bfloat16)
    group = width_all // N_TP
    out_groups = jnp.transpose(output.reshape(seq_len, N_TP, group), (1, 0, 2))
    weight_groups = out_weight.reshape(N_TP, group, width_all)

    def add_group(total, pieces):
        part = jnp.dot(pieces[0].astype(jnp.float32), pieces[1].astype(jnp.float32))
        part = lax.optimization_barrier(part.astype(jnp.bfloat16))
        return (total + part.astype(jnp.float32), None)
    total, unused = lax.scan(add_group, jnp.zeros((seq_len, width_all), jnp.float32), (out_groups, weight_groups))
    return total.astype(jnp.bfloat16)
```

```python
import jax
import jax.numpy as jnp
from jax import lax
from jax.experimental import pallas as pl
from jax.experimental.pallas import tpu as pltpu
from jax.sharding import PartitionSpec as P

MESH = pl.DeviceIdType.MESH
F32 = jnp.float32
BF16 = jnp.bfloat16

MODES = 16
WIDTH = 256
ROWS = 1024
SPAN = 512
SUB = 64
LANE = 128
CHUNK = 64
STEPS = ROWS // CHUNK
PIECE = WIDTH // 8


def kernel(
    q_hbm, k_hbm, v_hbm, res_ref, rate_ref, w_hbm, order_ref, out_ref,
    q_ref, k_ref, v_ref, w_ref, g_ref, y_ref, inner_ref, state_ref, table_ref,
    sa_ref, cs_ref, cr_ref, enter_ref, o_ref, p_ref, wp_ref, xs_ref, xr_ref, own_ref, zs_ref, zr_ref,
    load_sem, sa_s, sa_r, cb_s, cb_r, w1_s, w1_r, w2_s, w2_r, w3_s, w3_r,
    ag_s, ag_r, x_s, x_r, z_s, z_r,
):
    ctx = lax.axis_index("ctx")
    tp = lax.axis_index("tp")
    z = ctx // 8
    plane = ctx % 8
    x = tp // 4
    h = tp % 4
    pair = h + 1 - 2 * (h % 2)
    other = 3 - h

    def at_plane(to):
        return (z * 8 + to, tp)

    def at_z(to):
        return (to * 8 + plane, tp)

    def at_x(to):
        return (ctx, to * 4 + h)

    at_pair = (ctx, x * 4 + pair)
    at_other = (ctx, x * 4 + other)

    loads = [
        pltpu.make_async_copy(src, dst, load_sem.at[i])
        for i, (src, dst) in enumerate(((k_hbm, k_ref), (v_hbm, v_ref), (w_hbm, w_ref), (q_hbm, q_ref)))
    ]
    for load in loads:
        load.start()

    barrier = pltpu.get_barrier_semaphore()
    partners = [at_plane((plane + i) % 8) for i in range(1, 8)]
    partners += [at_z((z + i) % 8) for i in range(1, 8)]
    partners += [at_x((x + i) % 4) for i in range(1, 4)]
    partners += [at_pair, at_other]
    for partner in partners:
        pl.semaphore_signal(barrier, inc=1, device_id=partner, device_id_type=MESH)

    loads[0].wait()
    loads[1].wait()

    def gate(i, carry):
        rows = pl.ds(pl.multiple_of(i * 64, 64), 64)
        gated = (k_ref[rows].astype(F32) * v_ref[rows].astype(F32)).astype(BF16).astype(F32)
        g_ref[0, rows] = gated[:, :LANE]
        g_ref[1, rows] = gated[:, LANE:]
        return carry

    lax.fori_loop(0, ROWS // 64, gate, 0)

    def wide(row):
        return jnp.broadcast_to(row, (8, LANE))

    sub_index = lax.broadcasted_iota(jnp.int32, (8, LANE), 0)
    sub_float = sub_index.astype(F32)

    for u in range(2):
        lanes = pl.ds(u * LANE, LANE)
        decay = [wide(jnp.exp(-rate_ref[r : r + 1, lanes])) for r in range(MODES)]

        def advance(i, carry, u=u, decay=decay):
            carry = list(carry)
            for j in range(4):
                for s in range(2):
                    new = g_ref[u, pl.ds(s * SPAN + i * 4 + j, 8, stride=SUB), :]
                    for r in range(MODES):
                        carry[s * MODES + r] = carry[s * MODES + r] * decay[r] + new
            return tuple(carry)

        ends = lax.fori_loop(0, SUB // 4, advance, tuple(jnp.zeros((8, LANE), F32) for _ in range(2 * MODES)))
        for r in range(MODES):
            rate = rate_ref[r : r + 1, lanes]
            tail = jnp.exp(-(rate * SUB) * (7.0 - sub_float))
            for s in range(2):
                end = ends[s * MODES + r]
                inner_ref[u, s, r] = end
                state_ref[s, r : r + 1, lanes] = jnp.sum(end * tail, axis=0, keepdims=True)

    sa_ref[plane] = jnp.concatenate([state_ref[0], state_ref[1]], axis=0).astype(BF16)

    pl.semaphore_wait(barrier, len(partners))

    def plane_copy(i):
        return pltpu.make_async_remote_copy(
            src_ref=sa_ref.at[plane], dst_ref=sa_ref.at[plane],
            send_sem=sa_s.at[i - 1], recv_sem=sa_r.at[i - 1],
            device_id=at_plane((plane + i) % 8), device_id_type=MESH,
        )

    for i in range(1, 8):
        plane_copy(i).start()

    loads[2].wait()
    column = ((plane // 2) * 4 + (plane % 2) * (3 - pair) + (1 - plane % 2) * pair) * WIDTH
    rows_z = pl.ds(pl.multiple_of(z * PIECE, PIECE), PIECE)
    w1 = pltpu.make_async_remote_copy(
        src_ref=w_ref.at[rows_z, pl.ds(pl.multiple_of(column, WIDTH), WIDTH)],
        dst_ref=wp_ref.at[plane, rows_z],
        send_sem=w1_s, recv_sem=w1_r, device_id=at_pair, device_id_type=MESH,
    )
    w1.start()

    def w2(i):
        return pltpu.make_async_remote_copy(
            src_ref=wp_ref.at[plane, rows_z], dst_ref=wp_ref.at[plane, rows_z],
            send_sem=w2_s.at[i - 1], recv_sem=w2_r.at[i - 1],
            device_id=at_z((z + i) % 8), device_id_type=MESH,
        )

    def w3(i):
        return pltpu.make_async_remote_copy(
            src_ref=wp_ref.at[plane], dst_ref=wp_ref.at[plane],
            send_sem=w3_s.at[i - 1], recv_sem=w3_r.at[i - 1],
            device_id=at_plane((plane + i) % 8), device_id_type=MESH,
        )

    rate_span = rate_ref[...] * SPAN

    def tables(i, carry):
        for s in range(2):
            target = order_ref[(i * 8 + plane) * 2 + s]
            for j in range(16):
                gap = target - 1 - order_ref[z * 16 + j]
                live = jnp.where(gap >= 0, 1.0, 0.0).astype(F32)
                far = jnp.maximum(gap, 0).astype(F32)
                table_ref[i, s, j] = jnp.exp(rate_span * -far) * live
        return carry

    lax.fori_loop(0, 8, tables, 0)

    for i in range(1, 8):
        plane_copy(i).wait_recv()

    def combine(to):
        sums = []
        for s in range(2):
            total = jnp.zeros((MODES, WIDTH), F32)
            for j in range(16):
                half = pl.ds((j % 2) * MODES, MODES)
                total = total + table_ref[to, s, j] * sa_ref[j // 2, half].astype(F32)
            sums.append(total)
        return sums

    def z_copy(i):
        return pltpu.make_async_remote_copy(
            src_ref=cs_ref.at[i - 1], dst_ref=cr_ref.at[i - 1],
            send_sem=cb_s.at[i - 1], recv_sem=cb_r.at[i - 1],
            device_id=at_z((z + i) % 8), device_id_type=MESH,
        )

    def give(i, carry):
        sums = combine((z + i) % 8)
        cs_ref[i - 1] = jnp.concatenate(sums, axis=0).astype(BF16)
        z_copy(i).start()
        return carry

    lax.fori_loop(1, 8, give, 0)
    for s, total in enumerate(combine(z)):
        enter_ref[s] = total

    w1.wait_recv()
    for i in range(1, 8):
        w2(i).start()

    for u in range(2):
        lanes = pl.ds(u * LANE, LANE)
        decay = [wide(jnp.exp(-rate_ref[r : r + 1, lanes])) for r in range(MODES)]
        scale = [
            wide(res_ref[r : r + 1, lanes] * jnp.sqrt(2.0 * rate_ref[r : r + 1, lanes])) for r in range(MODES)
        ]
        for s in range(2):
            start = []
            for r in range(MODES):
                rate = rate_ref[r : r + 1, lanes]
                run = inner_ref[u, s, r]
                for shift in (1, 2, 4):
                    moved = jnp.where(sub_index >= shift, pltpu.roll(run, shift, 0), 0.0)
                    run = run + moved * jnp.exp(rate * float(-SUB * shift))
                start.append(jnp.where(sub_index >= 1, pltpu.roll(run, 1, 0), 0.0))

            def inside(i, carry, u=u, s=s, decay=decay, scale=scale):
                carry = list(carry)
                for j in range(4):
                    rows = pl.ds(s * SPAN + i * 4 + j, 8, stride=SUB)
                    new = g_ref[u, rows, :]
                    sums = [None] * 4
                    for r in range(MODES):
                        carry[r] = carry[r] * decay[r] + new
                        term = carry[r] * scale[r]
                        sums[r % 4] = term if sums[r % 4] is None else sums[r % 4] + term
                    y_ref[u, rows, :] = (sums[0] + sums[1]) + (sums[2] + sums[3])
                return tuple(carry)

            lax.fori_loop(0, SUB // 4, inside, tuple(start))

    for i in range(1, 8):
        w2(i).wait_recv()
    for i in range(1, 8):
        w3(i).start()

    for i in range(1, 8):
        z_copy(i).wait_recv()

    loads[3].wait()

    def ag(i):
        rows = pl.ds(pl.multiple_of(i * CHUNK, CHUNK), CHUNK)
        return pltpu.make_async_remote_copy(
            src_ref=o_ref.at[rows], dst_ref=p_ref.at[rows],
            send_sem=ag_s.at[i], recv_sem=ag_r.at[i], device_id=at_pair, device_id_type=MESH,
        )

    for s in range(2):
        total = enter_ref[s]
        for i in range(7):
            total = total + cr_ref[i, pl.ds(s * MODES, MODES)].astype(F32)
        total = total * (res_ref[...] * jnp.sqrt(2.0 * rate_ref[...]))
        enter_ref[s] = total
        for u in range(2):
            lanes = pl.ds(u * LANE, LANE)
            decay = []
            start = []
            for r in range(MODES):
                rate = rate_ref[r : r + 1, lanes]
                decay.append(wide(jnp.exp(-rate)))
                start.append(enter_ref[s, r : r + 1, lanes] * jnp.exp(-(rate * SUB) * sub_float))

            def outside(i, carry, u=u, s=s, decay=decay):
                carry = list(carry)
                for j in range(4):
                    rows = pl.ds(s * SPAN + i * 4 + j, 8, stride=SUB)
                    sums = [y_ref[u, rows, :], None, None, None]
                    for r in range(MODES):
                        carry[r] = carry[r] * decay[r]
                        sums[r % 4] = carry[r] if sums[r % 4] is None else sums[r % 4] + carry[r]
                    y_ref[u, rows, :] = (sums[0] + sums[1]) + (sums[2] + sums[3])
                return tuple(carry)

            lax.fori_loop(0, SUB // 4, outside, tuple(start))

        def send(i, carry):
            rows = pl.ds(pl.multiple_of(i * CHUNK, CHUNK), CHUNK)
            for u in range(2):
                lanes = pl.ds(u * LANE, LANE)
                mixed = y_ref[u, rows, :].astype(BF16).astype(F32)
                o_ref[rows, lanes] = (q_ref[rows, lanes].astype(F32) * mixed).astype(BF16)
            ag(i).start()
            return carry

        lax.fori_loop(s * STEPS // 2, (s + 1) * STEPS // 2, send, 0)

    for i in range(1, 8):
        w3(i).wait_recv()

    def x_copy(i, k):
        rows = pl.ds(pl.multiple_of(i * CHUNK, CHUNK), CHUNK)
        return pltpu.make_async_remote_copy(
            src_ref=xs_ref.at[k - 1, rows], dst_ref=xr_ref.at[k - 1, rows],
            send_sem=x_s.at[k - 1, i], recv_sem=x_r.at[k - 1, i],
            device_id=at_x((x + k) % 4), device_id_type=MESH,
        )

    def z_sum(i):
        rows = pl.ds(pl.multiple_of(i * CHUNK, CHUNK), CHUNK)
        return pltpu.make_async_remote_copy(
            src_ref=zs_ref.at[rows], dst_ref=zr_ref.at[rows],
            send_sem=z_s.at[i], recv_sem=z_r.at[i], device_id=at_other, device_id_type=MESH,
        )

    def part(rows, to, side):
        column = (to * 4 + (h if side == 0 else other)) * WIDTH
        mine = jnp.dot(
            o_ref[rows], w_ref[:, pl.ds(pl.multiple_of(column, WIDTH), WIDTH)], preferred_element_type=F32
        )
        theirs = jnp.dot(p_ref[rows], wp_ref[to * 2 + side], preferred_element_type=F32)
        return mine + theirs

    def step(i, carry):
        rows = pl.ds(pl.multiple_of(i * CHUNK, CHUNK), CHUNK)
        ag(i).wait_recv()
        for k in (2, 1, 3):
            to = (x + k) % 4
            for side in range(2):
                xs_ref[k - 1, rows, pl.ds(side * WIDTH, WIDTH)] = part(rows, to, side).astype(BF16)
            x_copy(i, k).start()
        mine = part(rows, x, 1)
        own_ref[rows] = part(rows, x, 0)
        for k in range(1, 4):
            x_copy(i, k).wait_recv()
        for k in range(3):
            mine = mine + xr_ref[k, rows, pl.ds(WIDTH, WIDTH)].astype(F32)
        zs_ref[rows] = mine.astype(BF16)
        z_sum(i).start()
        total = own_ref[rows]
        for k in range(3):
            total = total + xr_ref[k, rows, pl.ds(0, WIDTH)].astype(F32)
        own_ref[rows] = total
        return carry

    lax.fori_loop(0, STEPS, step, 0)

    def finish(i, carry):
        rows = pl.ds(pl.multiple_of(i * CHUNK, CHUNK), CHUNK)
        z_sum(i).wait_recv()
        out_ref[rows] = (own_ref[rows] + zr_ref[rows].astype(F32)).astype(BF16)
        return carry

    lax.fori_loop(0, STEPS, finish, 0)

    for i in range(1, 8):
        plane_copy(i).wait_send()
        z_copy(i).wait_send()
        w2(i).wait_send()
        w3(i).wait_send()
    w1.wait_send()

    def drain(i, carry):
        ag(i).wait_send()
        for k in range(1, 4):
            x_copy(i, k).wait_send()
        z_sum(i).wait_send()
        return carry

    lax.fori_loop(0, STEPS, drain, 0)


def local(queries, keys, values, residues, rates, out_weight, span_order):
    hbm = pl.BlockSpec(memory_space=pl.ANY)
    vmem = pl.BlockSpec(memory_space=pltpu.VMEM)
    smem = pl.BlockSpec(memory_space=pltpu.SMEM)
    dma = pltpu.SemaphoreType.DMA
    return pl.pallas_call(
        kernel,
        out_shape=jax.ShapeDtypeStruct((ROWS, WIDTH), BF16),
        in_specs=[hbm, hbm, hbm, vmem, vmem, hbm, smem],
        out_specs=vmem,
        scratch_shapes=[
            pltpu.VMEM((ROWS, WIDTH), BF16),
            pltpu.VMEM((ROWS, WIDTH), BF16),
            pltpu.VMEM((ROWS, WIDTH), BF16),
            pltpu.VMEM((WIDTH, 16 * WIDTH), BF16),
            pltpu.VMEM((2, ROWS, LANE), F32),
            pltpu.VMEM((2, ROWS, LANE), F32),
            pltpu.VMEM((2, 2, MODES, 8, LANE), F32),
            pltpu.VMEM((2, MODES, WIDTH), F32),
            pltpu.VMEM((8, 2, 16, MODES, WIDTH), F32),
            pltpu.VMEM((8, 2 * MODES, WIDTH), BF16),
            pltpu.VMEM((7, 2 * MODES, WIDTH), BF16),
            pltpu.VMEM((7, 2 * MODES, WIDTH), BF16),
            pltpu.VMEM((2, MODES, WIDTH), F32),
            pltpu.VMEM((ROWS, WIDTH), BF16),
            pltpu.VMEM((ROWS, WIDTH), BF16),
            pltpu.VMEM((8, WIDTH, WIDTH), BF16),
            pltpu.VMEM((3, ROWS, 2 * WIDTH), BF16),
            pltpu.VMEM((3, ROWS, 2 * WIDTH), BF16),
            pltpu.VMEM((ROWS, WIDTH), F32),
            pltpu.VMEM((ROWS, WIDTH), BF16),
            pltpu.VMEM((ROWS, WIDTH), BF16),
            dma((4,)),
            dma((7,)), dma((7,)), dma((7,)), dma((7,)),
            dma, dma,
            dma((7,)), dma((7,)), dma((7,)), dma((7,)),
            dma((STEPS,)), dma((STEPS,)),
            dma((3, STEPS)), dma((3, STEPS)),
            dma((STEPS,)), dma((STEPS,)),
        ],
        compiler_params=pltpu.CompilerParams(
            collective_id=0, has_side_effects=True, vmem_limit_bytes=50 * 2**20
        ),
    )(queries, keys, values, residues, rates, out_weight, span_order)


def solution(mesh):
    placed = (
        P("ctx", "tp"),
        P("ctx", "tp"),
        P("ctx", "tp"),
        P(None, "tp"),
        P(None, "tp"),
        P("tp", None),
        P(),
    )
    return jax.shard_map(
        local, mesh=mesh, in_specs=placed, out_specs=P("ctx", "tp"), check_vma=False
    )
```

```python
import jax
import jax.numpy as jnp
from jax import lax
from jax.experimental import pallas as pl
from jax.experimental.pallas import tpu as pltpu
from jax.sharding import PartitionSpec as P

MESH = pl.DeviceIdType.MESH
F32 = jnp.float32
BF16 = jnp.bfloat16

MODES = 16
WIDTH = 256
ROWS = 1024
SPAN = 512
SUB = 64
LANE = 128
CHUNK = 64
STEPS = ROWS // CHUNK
WINDOW = 2
PIECE = WIDTH // 8


def kernel(
    q_hbm, k_hbm, v_hbm, res_hbm, rate_hbm, w_hbm, order_hbm, out_ref,
    q_ref, k_ref, v_ref, w_ref, res_ref, rate_ref, order_ref, g_ref, y_ref, inner_ref, state_ref, table_ref,
    sa_ref, cs_ref, cr_ref, enter_ref, o_ref, p_ref, wp_ref, xs_ref, xr_ref, own_ref, zs_ref, zr_ref,
    load_sem, sa_s, sa_r, cb_s, cb_r, w1_s, w1_r, w2_s, w2_r, w3_s, w3_r, w4_s, w4_r,
    ag_s, ag_r, x_s, x_r, z_s, z_r,
):
    ctx = lax.axis_index("ctx")
    tp = lax.axis_index("tp")
    z = ctx // 8
    plane = ctx % 8
    x = tp // 4
    h = tp % 4
    pair = h + 1 - 2 * (h % 2)
    other = 3 - h
    window = WINDOW + jnp.maximum(z - 4, 3 - z)

    def at_plane(to):
        return (z * 8 + to, tp)

    def at_z(to):
        return (to * 8 + plane, tp)

    def at_x(to):
        return (ctx, to * 4 + h)

    at_pair = (ctx, x * 4 + pair)
    at_other = (ctx, x * 4 + other)

    loads = [
        pltpu.make_async_copy(src, dst, load_sem.at[i])
        for i, (src, dst) in enumerate((
            (k_hbm, k_ref), (v_hbm, v_ref), (rate_hbm, rate_ref), (res_hbm, res_ref),
            (order_hbm, order_ref), (q_hbm, q_ref), (w_hbm, w_ref),
        ))
    ]
    for load in loads:
        load.start()

    barrier = pltpu.get_barrier_semaphore()
    partners = [at_plane((plane + i) % 8) for i in range(1, 8)]
    partners += [at_z((z + i) % 8) for i in range(1, 8)]
    partners += [at_x((x + i) % 4) for i in range(1, 4)]
    partners += [at_pair, at_other]
    for partner in partners:
        pl.semaphore_signal(barrier, inc=1, device_id=partner, device_id_type=MESH)

    loads[0].wait()
    loads[1].wait()

    def gate(i, carry):
        rows = pl.ds(pl.multiple_of(i * 64, 64), 64)
        gated = (k_ref[rows].astype(F32) * v_ref[rows].astype(F32)).astype(BF16).astype(F32)
        g_ref[0, rows] = gated[:, :LANE]
        g_ref[1, rows] = gated[:, LANE:]
        return carry

    lax.fori_loop(0, ROWS // 64, gate, 0)

    def wide(row):
        return jnp.broadcast_to(row, (8, LANE))

    sub_index = lax.broadcasted_iota(jnp.int32, (8, LANE), 0)
    sub_float = sub_index.astype(F32)

    loads[2].wait()
    for u in range(2):
        lanes = pl.ds(u * LANE, LANE)
        decay = [wide(jnp.exp(-rate_ref[r : r + 1, lanes])) for r in range(MODES)]

        def advance(i, carry, u=u, decay=decay):
            carry = list(carry)
            for j in range(4):
                for s in range(2):
                    new = g_ref[u, pl.ds(s * SPAN + i * 4 + j, 8, stride=SUB), :]
                    for r in range(MODES):
                        carry[s * MODES + r] = carry[s * MODES + r] * decay[r] + new
            return tuple(carry)

        ends = lax.fori_loop(0, SUB // 4, advance, tuple(jnp.zeros((8, LANE), F32) for _ in range(2 * MODES)))
        for r in range(MODES):
            rate = rate_ref[r : r + 1, lanes]
            tail = jnp.exp(-(rate * SUB) * (7.0 - sub_float))
            for s in range(2):
                end = ends[s * MODES + r]
                inner_ref[u, s, r] = end
                state_ref[s, r : r + 1, lanes] = jnp.sum(end * tail, axis=0, keepdims=True)

    sa_ref[plane] = jnp.concatenate([state_ref[0], state_ref[1]], axis=0).astype(BF16)

    pl.semaphore_wait(barrier, len(partners))

    def plane_copy(i):
        return pltpu.make_async_remote_copy(
            src_ref=sa_ref.at[plane], dst_ref=sa_ref.at[plane],
            send_sem=sa_s.at[i - 1], recv_sem=sa_r.at[i - 1],
            device_id=at_plane((plane + i) % 8), device_id_type=MESH,
        )

    for i in range(1, 8):
        plane_copy(i).start()

    column = ((plane // 2) * 4 + (plane % 2) * (3 - pair) + (1 - plane % 2) * pair) * WIDTH
    rows_z = pl.ds(pl.multiple_of(z * PIECE, PIECE), PIECE)
    w1 = pltpu.make_async_remote_copy(
        src_ref=w_hbm.at[rows_z, pl.ds(pl.multiple_of(column, WIDTH), WIDTH)],
        dst_ref=wp_ref.at[plane, rows_z],
        send_sem=w1_s, recv_sem=w1_r, device_id=at_pair, device_id_type=MESH,
    )
    w1.start()

    def w2(i):
        return pltpu.make_async_remote_copy(
            src_ref=wp_ref.at[plane, rows_z], dst_ref=wp_ref.at[plane, rows_z],
            send_sem=w2_s.at[i - 1], recv_sem=w2_r.at[i - 1],
            device_id=at_z((z + i) % 8), device_id_type=MESH,
        )

    y = plane // 2
    core = plane % 2

    def w3(i):
        return pltpu.make_async_remote_copy(
            src_ref=wp_ref.at[plane], dst_ref=wp_ref.at[plane],
            send_sem=w3_s.at[i - 1], recv_sem=w3_r.at[i - 1],
            device_id=at_plane((y + i) % 4 * 2 + core), device_id_type=MESH,
        )

    def w4(i):
        piece = (y + 4 - i) % 4 * 2 + core
        return pltpu.make_async_remote_copy(
            src_ref=wp_ref.at[piece], dst_ref=wp_ref.at[piece],
            send_sem=w4_s.at[i], recv_sem=w4_r.at[i],
            device_id=at_plane(y * 2 + 1 - core), device_id_type=MESH,
        )

    loads[4].wait()
    rate_span = rate_ref[...] * SPAN

    def tables(i, carry):
        for s in range(2):
            target = order_ref[(i * 8 + plane) * 2 + s]
            for j in range(16):
                gap = target - 1 - order_ref[z * 16 + j]
                live = jnp.where(gap >= 0, 1.0, 0.0).astype(F32)
                far = jnp.maximum(gap, 0).astype(F32)
                table_ref[i, s, j] = jnp.exp(rate_span * -far) * live
        return carry

    lax.fori_loop(0, 8, tables, 0)

    for i in range(1, 8):
        plane_copy(i).wait_recv()

    def combine(to):
        sums = []
        for s in range(2):
            total = jnp.zeros((MODES, WIDTH), F32)
            for j in range(16):
                half = pl.ds((j % 2) * MODES, MODES)
                total = total + table_ref[to, s, j] * sa_ref[j // 2, half].astype(F32)
            sums.append(total)
        return sums

    def z_copy(i):
        return pltpu.make_async_remote_copy(
            src_ref=cs_ref.at[i - 1], dst_ref=cr_ref.at[i - 1],
            send_sem=cb_s.at[i - 1], recv_sem=cb_r.at[i - 1],
            device_id=at_z((z + i) % 8), device_id_type=MESH,
        )

    def give(i, carry):
        sums = combine((z + i) % 8)
        cs_ref[i - 1] = jnp.concatenate(sums, axis=0).astype(BF16)
        z_copy(i).start()
        return carry

    lax.fori_loop(1, 8, give, 0)
    for s, total in enumerate(combine(z)):
        enter_ref[s] = total

    w1.wait_recv()
    for i in range(1, 8):
        w2(i).start()

    loads[3].wait()
    for u in range(2):
        lanes = pl.ds(u * LANE, LANE)
        decay = [wide(jnp.exp(-rate_ref[r : r + 1, lanes])) for r in range(MODES)]
        scale = [
            wide(res_ref[r : r + 1, lanes] * jnp.sqrt(2.0 * rate_ref[r : r + 1, lanes])) for r in range(MODES)
        ]
        for s in range(2):
            start = []
            for r in range(MODES):
                rate = rate_ref[r : r + 1, lanes]
                run = inner_ref[u, s, r]
                for shift in (1, 2, 4):
                    moved = jnp.where(sub_index >= shift, pltpu.roll(run, shift, 0), 0.0)
                    run = run + moved * jnp.exp(rate * float(-SUB * shift))
                start.append(jnp.where(sub_index >= 1, pltpu.roll(run, 1, 0), 0.0))

            def inside(i, carry, u=u, s=s, decay=decay, scale=scale):
                carry = list(carry)
                for j in range(4):
                    rows = pl.ds(s * SPAN + i * 4 + j, 8, stride=SUB)
                    new = g_ref[u, rows, :]
                    sums = [None] * 4
                    for r in range(MODES):
                        carry[r] = carry[r] * decay[r] + new
                        term = carry[r] * scale[r]
                        sums[r % 4] = term if sums[r % 4] is None else sums[r % 4] + term
                    y_ref[u, rows, :] = (sums[0] + sums[1]) + (sums[2] + sums[3])
                return tuple(carry)

            lax.fori_loop(0, SUB // 4, inside, tuple(start))

    for i in range(1, 8):
        z_copy(i).wait_recv()

    loads[5].wait()

    def ag(i):
        rows = pl.ds(pl.multiple_of(i * CHUNK, CHUNK), CHUNK)
        return pltpu.make_async_remote_copy(
            src_ref=o_ref.at[rows], dst_ref=p_ref.at[rows],
            send_sem=ag_s.at[i], recv_sem=ag_r.at[i], device_id=at_pair, device_id_type=MESH,
        )

    for s in range(2):
        total = enter_ref[s]
        for i in range(7):
            total = total + cr_ref[i, pl.ds(s * MODES, MODES)].astype(F32)
        total = total * (res_ref[...] * jnp.sqrt(2.0 * rate_ref[...]))
        enter_ref[s] = total
        for u in range(2):
            lanes = pl.ds(u * LANE, LANE)
            decay = []
            start = []
            for r in range(MODES):
                rate = rate_ref[r : r + 1, lanes]
                decay.append(wide(jnp.exp(-rate)))
                start.append(enter_ref[s, r : r + 1, lanes] * jnp.exp(-(rate * SUB) * sub_float))

            def outside(i, carry, u=u, s=s, decay=decay):
                carry = list(carry)
                for j in range(4):
                    rows = pl.ds(s * SPAN + i * 4 + j, 8, stride=SUB)
                    sums = [y_ref[u, rows, :], None, None, None]
                    for r in range(MODES):
                        carry[r] = carry[r] * decay[r]
                        sums[r % 4] = carry[r] if sums[r % 4] is None else sums[r % 4] + carry[r]
                    y_ref[u, rows, :] = (sums[0] + sums[1]) + (sums[2] + sums[3])
                return tuple(carry)

            lax.fori_loop(0, SUB // 4, outside, tuple(start))

        def gated_out(i, carry):
            rows = pl.ds(pl.multiple_of(i * CHUNK, CHUNK), CHUNK)
            for u in range(2):
                lanes = pl.ds(u * LANE, LANE)
                mixed = y_ref[u, rows, :].astype(BF16).astype(F32)
                o_ref[rows, lanes] = (q_ref[rows, lanes].astype(F32) * mixed).astype(BF16)
            return carry

        lax.fori_loop(s * STEPS // 2, (s + 1) * STEPS // 2, gated_out, 0)
        if s == 0:
            for i in range(WINDOW + 3):

                @pl.when(i < window)
                def _(i=i):
                    ag(i).start()

    for i in range(1, 8):
        w2(i).wait_recv()
    for i in range(1, 4):
        w3(i).start()
    w4(0).start()

    for i in range(1, 4):
        w3(i).wait_recv()
        w4(i).start()
    for i in range(4):
        w4(i).wait_recv()
    loads[6].wait()

    def x_copy(i, k):
        rows = pl.ds(pl.multiple_of(i * CHUNK, CHUNK), CHUNK)
        return pltpu.make_async_remote_copy(
            src_ref=xs_ref.at[k - 1, rows], dst_ref=xr_ref.at[k - 1, rows],
            send_sem=x_s.at[k - 1, i], recv_sem=x_r.at[k - 1, i],
            device_id=at_x((x + k) % 4), device_id_type=MESH,
        )

    def z_sum(i):
        rows = pl.ds(pl.multiple_of(i * CHUNK, CHUNK), CHUNK)
        return pltpu.make_async_remote_copy(
            src_ref=zs_ref.at[rows], dst_ref=zr_ref.at[rows],
            send_sem=z_s.at[i], recv_sem=z_r.at[i], device_id=at_other, device_id_type=MESH,
        )

    def part(rows, to, side):
        column = (to * 4 + (h if side == 0 else other)) * WIDTH
        mine = jnp.dot(
            o_ref[rows], w_ref[:, pl.ds(pl.multiple_of(column, WIDTH), WIDTH)], preferred_element_type=F32
        )
        theirs = jnp.dot(p_ref[rows], wp_ref[to * 2 + side], preferred_element_type=F32)
        return mine + theirs

    def front(i):
        rows = pl.ds(pl.multiple_of(i * CHUNK, CHUNK), CHUNK)
        ag(i).wait_send()

        @pl.when(i + window < STEPS)
        def _():
            ag(i + window).start()

        ag(i).wait_recv()
        for k in (2, 1, 3):
            to = (x + k) % 4
            for side in range(2):
                xs_ref[k - 1, rows, pl.ds(side * WIDTH, WIDTH)] = part(rows, to, side).astype(BF16)
            x_copy(i, k).start()
        for side in range(2):
            own_ref[rows, pl.ds(side * WIDTH, WIDTH)] = part(rows, x, side)

    def back(i):
        rows = pl.ds(pl.multiple_of(i * CHUNK, CHUNK), CHUNK)
        for k in range(1, 4):
            x_copy(i, k).wait_recv()
        for side in (1, 0):
            lanes = pl.ds(side * WIDTH, WIDTH)
            total = own_ref[rows, lanes]
            for k in range(3):
                total = total + xr_ref[k, rows, lanes].astype(F32)
            if side == 1:
                zs_ref[rows] = total.astype(BF16)
                z_sum(i).start()
            else:
                own_ref[rows, lanes] = total

    def step(i, carry):
        front(i)
        back(i - 1)
        return carry

    front(jnp.int32(0))
    lax.fori_loop(1, STEPS, step, 0)
    back(jnp.int32(STEPS - 1))

    def finish(i, carry):
        rows = pl.ds(pl.multiple_of(i * CHUNK, CHUNK), CHUNK)
        z_sum(i).wait_recv()
        out_ref[rows] = (own_ref[rows, pl.ds(0, WIDTH)] + zr_ref[rows].astype(F32)).astype(BF16)
        return carry

    lax.fori_loop(0, STEPS, finish, 0)

    for i in range(1, 8):
        plane_copy(i).wait_send()
        z_copy(i).wait_send()
        w2(i).wait_send()
    for i in range(1, 4):
        w3(i).wait_send()
    for i in range(4):
        w4(i).wait_send()
    w1.wait_send()

    def drain(i, carry):
        for k in range(1, 4):
            x_copy(i, k).wait_send()
        z_sum(i).wait_send()
        return carry

    lax.fori_loop(0, STEPS, drain, 0)


def local(queries, keys, values, residues, rates, out_weight, span_order):
    hbm = pl.BlockSpec(memory_space=pl.ANY)
    vmem = pl.BlockSpec(memory_space=pltpu.VMEM)
    dma = pltpu.SemaphoreType.DMA
    return pl.pallas_call(
        kernel,
        out_shape=jax.ShapeDtypeStruct((ROWS, WIDTH), BF16),
        in_specs=[hbm] * 7,
        out_specs=vmem,
        scratch_shapes=[
            pltpu.VMEM((ROWS, WIDTH), BF16),
            pltpu.VMEM((ROWS, WIDTH), BF16),
            pltpu.VMEM((ROWS, WIDTH), BF16),
            pltpu.VMEM((WIDTH, 16 * WIDTH), BF16),
            pltpu.VMEM((MODES, WIDTH), F32),
            pltpu.VMEM((MODES, WIDTH), F32),
            pltpu.SMEM((128,), jnp.int32),
            pltpu.VMEM((2, ROWS, LANE), F32),
            pltpu.VMEM((2, ROWS, LANE), F32),
            pltpu.VMEM((2, 2, MODES, 8, LANE), F32),
            pltpu.VMEM((2, MODES, WIDTH), F32),
            pltpu.VMEM((8, 2, 16, MODES, WIDTH), F32),
            pltpu.VMEM((8, 2 * MODES, WIDTH), BF16),
            pltpu.VMEM((7, 2 * MODES, WIDTH), BF16),
            pltpu.VMEM((7, 2 * MODES, WIDTH), BF16),
            pltpu.VMEM((2, MODES, WIDTH), F32),
            pltpu.VMEM((ROWS, WIDTH), BF16),
            pltpu.VMEM((ROWS, WIDTH), BF16),
            pltpu.VMEM((8, WIDTH, WIDTH), BF16),
            pltpu.VMEM((3, ROWS, 2 * WIDTH), BF16),
            pltpu.VMEM((3, ROWS, 2 * WIDTH), BF16),
            pltpu.VMEM((ROWS, 2 * WIDTH), F32),
            pltpu.VMEM((ROWS, WIDTH), BF16),
            pltpu.VMEM((ROWS, WIDTH), BF16),
            dma((7,)),
            dma((7,)), dma((7,)), dma((7,)), dma((7,)),
            dma, dma,
            dma((7,)), dma((7,)), dma((3,)), dma((3,)), dma((4,)), dma((4,)),
            dma((STEPS,)), dma((STEPS,)),
            dma((3, STEPS)), dma((3, STEPS)),
            dma((STEPS,)), dma((STEPS,)),
        ],
        compiler_params=pltpu.CompilerParams(
            collective_id=0, has_side_effects=True, vmem_limit_bytes=62 * 2**20
        ),
    )(queries, keys, values, residues, rates, out_weight, span_order)


def solution(mesh):
    placed = (
        P("ctx", "tp"),
        P("ctx", "tp"),
        P("ctx", "tp"),
        P(None, "tp"),
        P(None, "tp"),
        P("tp", None),
        P(),
    )
    return jax.shard_map(
        local, mesh=mesh, in_specs=placed, out_specs=P("ctx", "tp"), check_vma=False
    )
```
